32 devices in a mesh: groups: 2 (over x), section: 16 (over z, y, core).
Axes of the slice: x: 2, y: 2, z: 4, core: 2. Of those that a mesh axis runs over, the one named last changes fastest.
Arguments:
- enc_rows: bfloat16 [2048, 6144], P('groups', 'section'), parts along dimension 0, may hold values from -6 to 6
- enc_gain: float32 [6144], replicated, may hold values from 0.5 to 1.5
- dec_input: bfloat16 [256, 6144], P('groups'), parts along dimension 0, may hold values from -6 to 6
- dec_gain: float32 [1, 6144], replicated, may hold values from 0.5 to 1.5
- w_query: bfloat16 [64, 6144, 128], P('section'), may hold values from -0.3125 to 0.3125
- w_keyval: bfloat16 [64, 6144, 256], P('section'), may hold values from -0.078125 to 0.078125
- w_out: bfloat16 [64, 128, 6144], P('section'), may hold values from -0.09375 to 0.09375
Outputs:
- decoded: bfloat16 [256, 6144], P('groups', 'section'), parts along dimension 0
The draws below stay inside these ranges and needn't reach their ends.
There are 2 independent parts, one for each index of `groups`. The reference program is written for one: setup_inputs(seed, part) draws one part's arguments, and reference() takes and returns one part's arrays. A program takes and returns all parts, laid end to end along the dimension named above; an argument that names none is the same for every part. Nothing has to cross between parts.
All inputs are finite; a program needn't handle non-finite values.
Results may differ from the reference program's by a relative error of at most 0.012.
Values may be sent and summed in bfloat16 or wider, within the bound.
No kernel may reach another device: no remote copies, remote signals or barrier semaphores. Data moves between devices by JAX's collectives and lax.ppermute only.
A program may use at most 128 MiB of HBM per device.

```python
import math
import jax
import jax.numpy as jnp
from jax import lax

D = 6144
HEADS = 64
HD = 128
ENC = 1024
TGT = 128
NL = 1


def block_levels(stream_key, extent, split, low, high):
    def one(dim, parts):
        heights = jax.random.uniform(jax.random.fold_in(jax.random.fold_in(stream_key, 6), dim), (parts,), jnp.float32, low / len(split), high / len(split))
        return jnp.repeat(jnp.exp(heights), extent[dim] // parts).reshape((-1,) + (1,) * (len(extent) - dim - 1))

    level = one(*split[0])
    for cut in split[1:]:
        level = level * one(*cut)
    return level


def noise(key, dims, scale, reach, shards=(), dtype=jnp.bfloat16):
    factor_of = block_levels(key, dims, shards, -0.22, 0.18) if shards else 1.0
    drawn = jax.random.normal(key, dims, jnp.float32) * scale * factor_of
    return jnp.minimum(jnp.maximum(drawn, -reach), reach).astype(dtype)


def setup_inputs(seed: int = 0, part: int = 0) -> dict:
    streams_of = jax.random.split(jax.random.key(seed), 8)
    part_splits = jax.random.split(jax.random.fold_in(streams_of[7], part), 8)
    enc_rows = noise(part_splits[0], (ENC, D), 1.0, 6.0, ((1, 16),))
    enc_gain = jnp.clip(1.0 + 0.1 * jax.random.normal(streams_of[1], (D,), jnp.float32), 0.5, 1.5)
    dec_input = noise(part_splits[2], (TGT, D), 1.0, 6.0)
    dec_gain = jnp.clip(1.0 + 0.1 * jax.random.normal(streams_of[3], (NL, D), jnp.float32), 0.5, 1.5)
    w_query = noise(streams_of[4], (NL * HEADS, D, HD), (D // 16) ** -0.5, 0.3125, ((0, 16),))
    w_keyval = noise(streams_of[5], (NL * HEADS, D, 2 * HD), D ** -0.5, 0.078125, ((0, 16),))
    w_out = noise(streams_of[6], (NL * HEADS, HD, D), (HEADS * HD // 2) ** -0.5, 0.09375, ((0, 16),))
    return {"enc_rows": enc_rows, "enc_gain": enc_gain, "dec_input": dec_input, "dec_gain": dec_gain, "w_query": w_query, "w_keyval": w_keyval, "w_out": w_out}


epsilon = 1e-06

def rms_scaled(values, gain):
    return values * lax.rsqrt(lax.optimization_barrier(jnp.mean(values * values, axis=-1, keepdims=True)) + epsilon) * gain

def reference(enc_rows, enc_gain, dec_input, dec_gain, w_query, w_keyval, w_out):
    encoded = rms_scaled(enc_rows.astype(jnp.float32), enc_gain).astype(jnp.bfloat16)
    state = dec_input.astype(jnp.float32)
    score_scale = 1.0 / math.sqrt(HD)
    for layer_idx in range(NL):
        normed = rms_scaled(state, dec_gain[layer_idx]).astype(jnp.bfloat16)

        def one_head(running, weights):
            query_w, keyval_w, output_w = weights
            queries = (jnp.dot(normed, query_w, preferred_element_type=jnp.float32) * score_scale).astype(jnp.bfloat16)
            keyvals = jnp.dot(encoded, keyval_w, preferred_element_type=jnp.float32).astype(jnp.bfloat16)
            scores = jnp.dot(queries, keyvals[:, :HD].T, preferred_element_type=jnp.float32)
            weights_bf = jax.nn.softmax(scores, axis=-1).astype(jnp.bfloat16)
            context = jnp.dot(weights_bf, keyvals[:, HD:], preferred_element_type=jnp.float32).astype(jnp.bfloat16)
            return (running + jnp.dot(context, output_w, preferred_element_type=jnp.float32), None)
        first_head = layer_idx * HEADS
        running, unused = lax.scan(one_head, jnp.zeros((TGT, D), jnp.float32), (w_query[first_head:first_head + HEADS], w_keyval[first_head:first_head + HEADS], w_out[first_head:first_head + HEADS]))
        state = state + running
    return state.astype(jnp.bfloat16)
```

```python
import functools
import math

import jax
import jax.numpy as jnp
import numpy as np
from jax import lax
from jax.experimental import pallas as pl
from jax.experimental.pallas import tpu as pltpu
from jax.sharding import PartitionSpec as P

epsilon = 1e-06
MAX_RING = 8
VMEM_MIB = 60
STEP_MIB = 48
TILE = 16


def rms_scaled(values, gain):
    return values * lax.rsqrt(jnp.mean(values * values, axis=-1, keepdims=True) + epsilon) * gain


def ring_order(chips):
    return list(range(0, chips, 2)) + list(range(1, chips, 2))[::-1]


def params(mib):
    return pltpu.CompilerParams(vmem_limit_bytes=mib * 2**20)


def anywhere(count):
    return [pl.BlockSpec(memory_space=pl.ANY)] * count


def prepare_kernel(rows_ref, gain_ref, *halves):
    cols = rows_ref.shape[1]
    for which, half_ref in enumerate(halves):
        rows = half_ref.shape[0] - TILE
        values = rows_ref[which * rows : (which + 1) * rows, :].astype(jnp.float32)
        half_ref[:rows, :] = (values * gain_ref[...]).astype(jnp.bfloat16)
        squares = values * values
        high = squares.astype(jnp.bfloat16)
        low = (squares - high.astype(jnp.float32)).astype(jnp.bfloat16)
        ones = jnp.ones((8, cols), jnp.bfloat16)
        sums = sum(
            lax.dot_general(ones, part, (((1,), (1,)), ((), ())), preferred_element_type=jnp.float32)
            for part in (high, low)
        )[:1]
        terms = []
        for _ in range(3):
            terms.append(sums.astype(jnp.bfloat16).astype(jnp.float32))
            sums = sums - terms[-1]
        per = -(-rows // cols)
        lines = []
        for term in terms:
            for line in range(per):
                part = term[:, line * cols : min(rows, (line + 1) * cols)]
                if part.shape[1] < cols:
                    part = jnp.concatenate([part, jnp.zeros((1, cols - part.shape[1]), jnp.float32)], axis=1)
                lines.append(part)
        lines.append(jnp.zeros((TILE - len(lines), cols), jnp.float32))
        half_ref[rows:, :] = jnp.concatenate(lines, axis=0).astype(jnp.bfloat16)


def prepare(enc_rows, gain_share):
    rows, cols = enc_rows.shape
    return pl.pallas_call(
        prepare_kernel,
        out_shape=[jax.ShapeDtypeStruct((rows // 2 + TILE, cols), jnp.bfloat16)] * 2,
        compiler_params=params(VMEM_MIB),
        name="prepare",
    )(enc_rows, gain_share[None, :])


def lane_sums(tile, rows):
    cols = tile.shape[1]
    per = -(-rows // cols)
    lines = []
    for line in range(per):
        term = sum(tile[k * per + line : k * per + line + 1, :] for k in range(3))
        lines.append(term[:, : min(cols, rows - line * cols)])
    return jnp.concatenate(lines, axis=1)


def start_blocks(index_ref, slots, pieces, w_ref, rows_at, tiles, weights, rows_sem, tiles_sem, weights_sem):
    heads = weights.shape[0]
    rows, features = rows_at.shape[0], tiles.shape[2]
    row_copies, tile_copies, weight_copies = [], [], []
    for slot in range(slots):
        columns = pl.ds(slot * features, features)
        at = 0
        for piece in pieces[slot]:
            size = min(piece.shape[0], rows - at)
            source = piece.at[pl.ds(0, size), :]
            target = rows_at.at[pl.ds(at, size), columns]
            row_copies.append(pltpu.make_async_copy(source, target, rows_sem.at[len(row_copies)]))
            at += size
        source = pieces[slot][-1].at[pl.ds(pieces[slot][-1].shape[0] - TILE, TILE), :]
        tile_copies.append(pltpu.make_async_copy(source, tiles.at[slot], tiles_sem.at[slot]))
    for head in range(heads):
        group = []
        for slot in range(slots):
            source = w_ref.at[head, pl.ds(pl.multiple_of(index_ref[slot] * features, features), features), :]
            target = weights.at[head, pl.ds(slot * features, features), :]
            group.append(pltpu.make_async_copy(source, target, weights_sem.at[head, slot]))
        weight_copies.append(group)
    return row_copies, tile_copies, weight_copies


def block_scratch(slots, rows, features, heads, pair):
    pieces = sum(slots)
    return [
        pltpu.VMEM((rows, features * len(slots)), jnp.bfloat16),
        pltpu.VMEM((len(slots), TILE, features), jnp.bfloat16),
        pltpu.VMEM((heads, features * len(slots), pair), jnp.bfloat16),
        pltpu.SemaphoreType.DMA((pieces,)),
        pltpu.SemaphoreType.DMA((len(slots),)),
        pltpu.SemaphoreType.DMA((heads, len(slots))),
    ]


def start_all(copies):
    for copy in copies:
        copy.start()


def wait_all(copies):
    for copy in copies:
        copy.wait()


def sum_kernel(slots, first, index_ref, *refs):
    refs = list(refs)
    pieces = [[refs.pop(0) for _ in range(count)] for count in slots]
    w_ref = refs.pop(0)
    sum_in, tile_in = (None, None) if first else (refs.pop(0), refs.pop(0))
    sum_out, tile_out, rows_at, tiles, weights, rows_sem, tiles_sem, weights_sem = refs
    heads = weights.shape[0]
    row_copies, tile_copies, weight_copies = start_blocks(
        index_ref, len(slots), pieces, w_ref, rows_at, tiles, weights, rows_sem, tiles_sem, weights_sem
    )
    start_all(row_copies)
    start_all(weight_copies[0])
    start_all(tile_copies)
    wait_all(row_copies)
    for head in range(heads):
        if head + 1 < heads:
            start_all(weight_copies[head + 1])
        wait_all(weight_copies[head])
        term = jnp.dot(rows_at[...], weights[head], preferred_element_type=jnp.float32)
        sum_out[head] = term if first else sum_in[head] + term
    wait_all(tile_copies)
    squares = sum(tiles[slot].astype(jnp.float32) for slot in range(len(slots)))
    tile_out[...] = squares if first else tile_in[...] + squares


def sum_step(index, slots, w_keyval, rows, carried=None):
    heads, width, pair = w_keyval.shape
    features = slots[0][0].shape[1]
    counts = tuple(len(parts) for parts in slots)
    pieces = [piece for parts in slots for piece in parts]
    operands = pieces + [w_keyval] + list(carried or ())
    whole = pl.BlockSpec(memory_space=pltpu.VMEM)
    depth = features * len(slots)
    aliases = {} if carried is None else {len(pieces) + 2: 0, len(pieces) + 3: 1}
    return pl.pallas_call(
        functools.partial(sum_kernel, counts, carried is None),
        out_shape=[pltpu.VMEM((heads, rows, pair), jnp.float32), pltpu.VMEM((TILE, features), jnp.float32)],
        grid_spec=pltpu.PrefetchScalarGridSpec(
            num_scalar_prefetch=1,
            grid=(),
            in_specs=anywhere(len(pieces) + 1) + [whole] * (len(operands) - len(pieces) - 1),
            out_specs=[whole] * 2,
            scratch_shapes=block_scratch(counts, rows, features, heads, pair),
        ),
        input_output_aliases=aliases,
        compiler_params=params(STEP_MIB),
        cost_estimate=pl.CostEstimate(
            flops=2 * rows * depth * heads * pair, bytes_accessed=2 * depth * heads * pair, transcendentals=0
        ),
        name="sum_step",
    )(index, *operands)


def attend_kernel(slots, merging, width, index_ref, *refs):
    refs = list(refs)
    pieces = [[refs.pop(0) for _ in range(count)] for count in slots]
    w_ref, sum_in, tile_in, query_ref = [refs.pop(0) for _ in range(4)]
    if merging:
        context_in, top_in, total_in, w_out_ref = [refs.pop(0) for _ in range(4)]
        theirs_ref, mine_ref = refs.pop(0), refs.pop(0)
    else:
        context_out, top_out, total_out = [refs.pop(0) for _ in range(3)]
    rows_at, tiles, weights, rows_sem, tiles_sem, weights_sem = [refs.pop(0) for _ in range(6)]
    heads, rows, pair = sum_in.shape
    size = pair // 2
    row_copies, tile_copies, weight_copies = start_blocks(
        index_ref, len(slots), pieces, w_ref, rows_at, tiles, weights, rows_sem, tiles_sem, weights_sem
    )
    start_all(row_copies)
    start_all(tile_copies)
    for head in range(heads):
        start_all(weight_copies[head])
    if merging:
        w_out_at, out_sem, merged = refs
        out_copies = [
            pltpu.make_async_copy(w_out_ref.at[head], w_out_at.at[head], out_sem.at[head]) for head in range(heads)
        ]
        start_all(out_copies)
    wait_all(tile_copies)
    squares = sum((tiles[slot].astype(jnp.float32) for slot in range(len(slots))), tile_in[...])
    inverse = lax.rsqrt(lane_sums(squares, rows) / width + epsilon)
    wait_all(row_copies)
    for head in range(heads):
        wait_all(weight_copies[head])
        keyvals = (
            sum_in[head] + jnp.dot(rows_at[...], weights[head], preferred_element_type=jnp.float32)
        ).astype(jnp.bfloat16)
        scores = inverse * lax.dot_general(
            query_ref[head], keyvals[:, :size], (((1,), (1,)), ((), ())), preferred_element_type=jnp.float32
        )
        top = jnp.max(scores, axis=1, keepdims=True)
        weight = jnp.exp(scores - top)
        norm = jnp.sum(weight, axis=1, keepdims=True)
        context = jnp.dot(
            (weight * inverse).astype(jnp.bfloat16), keyvals[:, size:], preferred_element_type=jnp.float32
        )
        if not merging:
            context_out[head] = context
            top_out[head] = jnp.broadcast_to(top, top_out.shape[1:])
            total_out[head] = jnp.broadcast_to(norm, total_out.shape[1:])
            continue
        other_top, other_norm = top_in[head][:, :1], total_in[head][:, :1]
        highest = jnp.maximum(top, other_top)
        left, right = jnp.exp(top - highest), jnp.exp(other_top - highest)
        whole = left * norm + right * other_norm
        joined = context * (left / whole) + context_in[head] * (right / whole)
        merged[:, head * size : (head + 1) * size] = joined.astype(jnp.bfloat16)
    if not merging:
        return
    wait_all(out_copies)
    count, _, cols = mine_ref.shape
    for part, target in enumerate((theirs_ref, mine_ref)):
        @pl.loop(0, count)
        def _(step):
            block = index_ref[len(slots) + part * count + step]
            columns = pl.ds(pl.multiple_of(block * cols, cols), cols)
            out_part = w_out_at[:, :, columns].reshape(heads * size, cols)
            value = jnp.dot(merged[...], out_part, preferred_element_type=jnp.float32)
            target[step] = value.astype(target.dtype)


def attend(index, slots, w_keyval, carried, queries, other=None, w_out=None, blocks=0, cols=0):
    heads, width, pair = w_keyval.shape
    rows = carried[0].shape[1]
    features = slots[0][0].shape[1]
    counts = tuple(len(parts) for parts in slots)
    target, size = queries.shape[1:]
    pieces = [piece for parts in slots for piece in parts]
    operands = pieces + [w_keyval, *carried, queries]
    whole = pl.BlockSpec(memory_space=pltpu.VMEM)
    in_specs = anywhere(len(pieces) + 1) + [whole] * 3
    depth = features * len(slots)
    scratch = block_scratch(counts, rows, features, heads, pair)
    merging = other is not None
    if merging:
        operands += list(other) + [w_out]
        in_specs += [whole] * 3 + anywhere(1)
        scratch += [
            pltpu.VMEM(w_out.shape, w_out.dtype),
            pltpu.SemaphoreType.DMA((heads,)),
            pltpu.VMEM((target, heads * size), jnp.bfloat16),
        ]
        out_shape = [
            jax.ShapeDtypeStruct((blocks, target, cols), jnp.bfloat16),
            pltpu.VMEM((blocks, target, cols), jnp.float32),
        ]
    else:
        out_shape = [pltpu.VMEM((heads, target, last), jnp.float32) for last in (size, 128, 128)]
    return pl.pallas_call(
        functools.partial(attend_kernel, counts, merging, width),
        out_shape=out_shape,
        grid_spec=pltpu.PrefetchScalarGridSpec(
            num_scalar_prefetch=1,
            grid=(),
            in_specs=in_specs,
            out_specs=[whole] * len(out_shape),
            scratch_shapes=scratch,
        ),
        compiler_params=params(STEP_MIB),
        cost_estimate=pl.CostEstimate(
            flops=2 * rows * depth * heads * pair, bytes_accessed=2 * depth * heads * pair, transcendentals=0
        ),
        name="attend",
    )(index, *operands)


def add_kernel(mine_ref, other_ref, *outs):
    for block, out in enumerate(outs):
        out[...] = (mine_ref[block] + other_ref[block].astype(jnp.float32)).astype(out.dtype)


def add_blocks(mine, other):
    count, target, cols = mine.shape
    return pl.pallas_call(
        add_kernel,
        out_shape=[
            jax.ShapeDtypeStruct((target, cols), jnp.float32 if block == 0 else jnp.bfloat16)
            for block in range(count)
        ],
        compiler_params=params(VMEM_MIB),
        name="add_blocks",
    )(mine, other)


def ring_body(enc_rows, enc_gain, dec_input, dec_gain, w_query, w_keyval, w_out):
    sections = lax.axis_size("section")
    position = lax.axis_index("section")
    chips = sections // 2
    ring = ring_order(chips)
    place = {chip: k for k, chip in enumerate(ring)}
    width = dec_input.shape[1]
    cols = width // sections
    head_size = w_query.shape[2]
    score_scale = 1.0 / math.sqrt(head_size)
    far = chips // 2

    def at(chip, offset):
        return ring[(place[chip] + offset) % chips]

    def hop(values, offset):
        pairs = [(2 * chip + core, 2 * at(chip, offset) + core) for chip in range(chips) for core in range(2)]
        return lax.ppermute(values, "section", pairs)

    def swap(values):
        return lax.ppermute(values, "section", [(s, s ^ 1) for s in range(sections)])

    table = []
    for s in range(sections):
        chip, core = divmod(s, 2)
        row = [s, s ^ 1]
        for step in range(1, far):
            for side in (core, 1 - core):
                row += [2 * at(chip, -step) + side, 2 * at(chip, step) + side]
        row += [2 * at(chip, far) + core, 2 * at(chip, far) + 1 - core]
        for side in (1 - core, core):
            row += [2 * at(chip, k) + side for k in range(chips)]
        table.append(row)
    row = lax.dynamic_slice_in_dim(jnp.asarray(np.array(table, np.int32)), position, 1, 0)[0]
    first_slot = [0] + [2 + 4 * step for step in range(far)]

    half_rows = enc_rows.shape[0] // 2
    own = prepare(enc_rows, lax.dynamic_slice_in_dim(enc_gain, position * cols, cols, 0))
    state = dec_input.astype(jnp.float32)
    normed = rms_scaled(state, dec_gain[0]).astype(jnp.bfloat16)
    queries = (
        jnp.einsum("td,hdk->htk", normed, w_query, preferred_element_type=jnp.float32) * score_scale
    ).astype(jnp.bfloat16)

    carried = [None, None]
    slots = [[(half,), (swap(half),)] for half in own]
    held = [(half, half) for half in own]
    flying = [(hop(half, 1), hop(half, -1)) for half in own]
    token = queries
    for phase in range(2 * far):
        step, which = phase // 2 + 1, phase % 2
        *arrived, token = lax.optimization_barrier((*flying[phase], token))
        if step + 1 < far:
            flying.append((hop(arrived[0], 1), hop(arrived[1], -1)))
        elif step + 1 == far:
            cut = half_rows // 2
            flying.append((hop(arrived[0][:cut], 1), hop(arrived[1][cut:], -1)))
        other = [swap(part) for part in arrived]
        if step < far:
            received = [(part,) for part in arrived + other]
        else:
            received = [tuple(arrived), tuple(other)]
        slots.append(received)
        if phase == 0:
            todo, half, begin = slots[0], 0, 0
        elif phase == 2:
            todo, half, begin = slots[1] + slots[3], 1, 0
        else:
            todo, half, begin = slots[phase + 1], 1 - which, first_slot[(phase + 1) // 2]
        if phase < 2 * far - 1:
            carried[half] = sum_step(row[begin : begin + len(todo)], todo, w_keyval, half_rows, carried[half])
            token = carried[half][1]
    last = first_slot[far]
    first = attend(row[last : last + 2], slots[2 * far], w_keyval, carried[0], queries)
    theirs, mine = attend(row[last:], slots[2 * far + 1], w_keyval, carried[1], queries, first, w_out, chips, cols)
    blocks = add_blocks(mine, swap(theirs))
    share = lax.dynamic_slice_in_dim(dec_input, position * cols, cols, 1).astype(jnp.float32)
    total = share + blocks[0]
    for k in range(1, chips):
        total = total + hop(blocks[k], k).astype(jnp.float32)
    return total.astype(jnp.bfloat16)


def general_body(enc_rows, enc_gain, dec_input, dec_gain, w_query, w_keyval, w_out):
    sections = lax.axis_size("section")
    position = lax.axis_index("section")
    layers = dec_gain.shape[0]
    target_rows = dec_input.shape[0]
    model_width = dec_input.shape[1]
    head_size = w_query.shape[2]
    score_scale = 1.0 / math.sqrt(head_size)
    my_layer = position // (sections // layers)
    whole_rows = lax.all_gather(enc_rows, "section", axis=1, tiled=True)
    encoded = rms_scaled(whole_rows.astype(jnp.float32), enc_gain).astype(jnp.bfloat16)
    keyvals = jnp.einsum(
        "rd,hdk->rhk", encoded, w_keyval, preferred_element_type=jnp.float32
    ).astype(jnp.bfloat16)
    key_rows = keyvals[:, :, :head_size]
    value_rows = keyvals[:, :, head_size:]

    def head_context(normed):
        queries = (
            jnp.einsum("td,hdk->htk", normed, w_query, preferred_element_type=jnp.float32)
            * score_scale
        ).astype(jnp.bfloat16)
        scores = jnp.einsum("htk,rhk->htr", queries, key_rows, preferred_element_type=jnp.float32)
        weights_bf = jax.nn.softmax(scores, axis=-1).astype(jnp.bfloat16)
        return jnp.einsum(
            "htr,rhk->htk", weights_bf, value_rows, preferred_element_type=jnp.float32
        ).astype(jnp.bfloat16)

    col_share = model_width // sections
    col_start = position * col_share
    state_share = lax.dynamic_slice_in_dim(dec_input, col_start, col_share, 1).astype(jnp.float32)
    for layer_idx in range(layers):
        squares = lax.psum(jnp.sum(state_share * state_share, axis=1), "section")
        gain_share = lax.dynamic_slice_in_dim(dec_gain[layer_idx], col_start, col_share, 0)
        inverse = lax.rsqrt(squares / model_width + epsilon)
        normed_share = (state_share * inverse[:, None] * gain_share).astype(jnp.bfloat16)
        normed = lax.all_gather(normed_share, "section", axis=1, tiled=True)

        def project_out(normed_in):
            return jnp.einsum(
                "htk,hkd->td", head_context(normed_in), w_out, preferred_element_type=jnp.float32
            )

        def skipped(normed_in):
            return jnp.zeros((target_rows, model_width), jnp.float32)

        state_share = state_share + lax.psum_scatter(
            lax.cond(my_layer == layer_idx, project_out, skipped, normed),
            "section",
            scatter_dimension=1,
            tiled=True,
        )
    return state_share.astype(jnp.bfloat16)


def body(enc_rows, enc_gain, dec_input, dec_gain, w_query, w_keyval, w_out):
    chips, odd = divmod(lax.axis_size("section"), 2)
    ringed = not odd and 4 <= chips <= MAX_RING and chips & (chips - 1) == 0 and dec_gain.shape[0] == 1
    chosen = ring_body if ringed else general_body
    return chosen(enc_rows, enc_gain, dec_input, dec_gain, w_query, w_keyval, w_out)


def solution(mesh):
    in_specs = (
        P("groups", "section"),
        P(),
        P("groups", None),
        P(),
        P("section", None, None),
        P("section", None, None),
        P("section", None, None),
    )
    out_specs = P("groups", "section")
    return jax.shard_map(body, mesh=mesh, in_specs=in_specs, out_specs=out_specs, check_vma=False)
```

```python
import functools
import math

import jax
import jax.numpy as jnp
import numpy as np
from jax import lax
from jax.experimental import pallas as pl
from jax.experimental.pallas import tpu as pltpu
from jax.sharding import PartitionSpec as P

epsilon = 1e-06
MAX_RING = 8
SMALL_MIB = 16
PARTS = 2
STEP_MIB = 48
TILE = 16


def rms_scaled(values, gain):
    return values * lax.rsqrt(jnp.mean(values * values, axis=-1, keepdims=True) + epsilon) * gain


def ring_order(chips):
    return list(range(0, chips, 2)) + list(range(1, chips, 2))[::-1]


def params(mib):
    return pltpu.CompilerParams(vmem_limit_bytes=mib * 2**20)


def anywhere(count):
    return [pl.BlockSpec(memory_space=pl.ANY)] * count


def prepare_kernel(index_ref, rows_ref, gain_ref, *refs):
    half_ref = refs[-1]
    rows, cols = rows_ref.shape
    values = rows_ref[...].astype(jnp.float32)
    half_ref[:rows, :] = (values * gain_ref[...]).astype(jnp.bfloat16)
    squares = values * values
    high = squares.astype(jnp.bfloat16)
    low = (squares - high.astype(jnp.float32)).astype(jnp.bfloat16)
    ones = jnp.ones((8, cols), jnp.bfloat16)
    sums = sum(
        lax.dot_general(ones, part, (((1,), (1,)), ((), ())), preferred_element_type=jnp.float32)
        for part in (high, low)
    )[:1]
    terms = []
    for _ in range(3):
        terms.append(sums.astype(jnp.bfloat16).astype(jnp.float32))
        sums = sums - terms[-1]
    lines = []
    for term in terms:
        for line in range(-(-rows // cols)):
            part = term[:, line * cols : min(rows, (line + 1) * cols)]
            if part.shape[1] < cols:
                part = jnp.concatenate([part, jnp.zeros((1, cols - part.shape[1]), jnp.float32)], axis=1)
            lines.append(part)
    lines.append(jnp.zeros((TILE - len(lines), cols), jnp.float32))
    half_ref[rows:, :] = jnp.concatenate(lines, axis=0).astype(jnp.bfloat16)


def prepare(position, enc_rows, enc_gain, which, before=()):
    rows, cols = enc_rows.shape[0] // 2, enc_rows.shape[1]
    return pl.pallas_call(
        prepare_kernel,
        out_shape=jax.ShapeDtypeStruct((rows + TILE, cols), jnp.bfloat16),
        grid_spec=pltpu.PrefetchScalarGridSpec(
            num_scalar_prefetch=1,
            grid=(1,),
            in_specs=[
                pl.BlockSpec((rows, cols), lambda g, i: (which, 0)),
                pl.BlockSpec((1, cols), lambda g, i: (0, i[0])),
            ]
            + anywhere(len(before)),
            out_specs=pl.BlockSpec((rows + TILE, cols), lambda g, i: (0, 0)),
        ),
        compiler_params=params(SMALL_MIB),
        name="prepare",
    )(position[None], enc_rows, enc_gain[None, :], *before)


def lane_sums(tile, rows):
    cols = tile.shape[1]
    per = -(-rows // cols)
    lines = []
    for line in range(per):
        term = sum(tile[k * per + line : k * per + line + 1, :] for k in range(3))
        lines.append(term[:, : min(cols, rows - line * cols)])
    return jnp.concatenate(lines, axis=1)


def start_blocks(index_ref, slots, pieces, w_ref, rows_at, tiles, weights, rows_sem, tiles_sem, weights_sem):
    heads = weights.shape[0]
    rows, features = rows_at.shape[0], tiles.shape[2]
    row_copies, tile_copies, weight_copies = [], [], []
    for slot in range(slots):
        columns = pl.ds(slot * features, features)
        at = 0
        for piece in pieces[slot]:
            size = min(piece.shape[0], rows - at)
            source = piece.at[pl.ds(0, size), :]
            target = rows_at.at[pl.ds(at, size), columns]
            row_copies.append(pltpu.make_async_copy(source, target, rows_sem.at[len(row_copies)]))
            at += size
        source = pieces[slot][-1].at[pl.ds(pieces[slot][-1].shape[0] - TILE, TILE), :]
        tile_copies.append(pltpu.make_async_copy(source, tiles.at[slot], tiles_sem.at[slot]))
    for head in range(heads):
        group = []
        for slot in range(slots):
            source = w_ref.at[head, pl.ds(pl.multiple_of(index_ref[slot] * features, features), features), :]
            target = weights.at[head, pl.ds(slot * features, features), :]
            group.append(pltpu.make_async_copy(source, target, weights_sem.at[head, slot]))
        weight_copies.append(group)
    return row_copies, tile_copies, weight_copies


def block_scratch(slots, rows, features, heads, pair):
    pieces = sum(slots)
    return [
        pltpu.VMEM((rows, features * len(slots)), jnp.bfloat16),
        pltpu.VMEM((len(slots), TILE, features), jnp.bfloat16),
        pltpu.VMEM((heads, features * len(slots), pair), jnp.bfloat16),
        pltpu.SemaphoreType.DMA((pieces,)),
        pltpu.SemaphoreType.DMA((len(slots),)),
        pltpu.SemaphoreType.DMA((heads, len(slots))),
    ]


def start_all(copies):
    for copy in copies:
        copy.start()


def wait_all(copies):
    for copy in copies:
        copy.wait()


def sum_kernel(slots, first, index_ref, *refs):
    refs = list(refs)
    pieces = [[refs.pop(0) for _ in range(count)] for count in slots]
    w_ref = refs.pop(0)
    sum_in, tile_in = (None, None) if first else (refs.pop(0), refs.pop(0))
    sum_out, tile_out, rows_at, tiles, weights, rows_sem, tiles_sem, weights_sem = refs
    heads = weights.shape[0]
    row_copies, tile_copies, weight_copies = start_blocks(
        index_ref, len(slots), pieces, w_ref, rows_at, tiles, weights, rows_sem, tiles_sem, weights_sem
    )
    start_all(row_copies)
    for copies in weight_copies:
        start_all(copies)
    start_all(tile_copies)
    wait_all(row_copies)
    for pair in range(0, heads, 2):
        both = range(pair, min(pair + 2, heads))
        for head in both:
            wait_all(weight_copies[head])
        for head in both:
            term = jnp.dot(rows_at[...], weights[head], preferred_element_type=jnp.float32)
            sum_out[head] = term if first else sum_in[head] + term
    wait_all(tile_copies)
    squares = sum(tiles[slot].astype(jnp.float32) for slot in range(len(slots)))
    tile_out[...] = squares if first else tile_in[...] + squares


def sum_step(index, slots, w_keyval, rows, carried=None):
    heads, width, pair = w_keyval.shape
    features = slots[0][0].shape[1]
    counts = tuple(len(parts) for parts in slots)
    pieces = [piece for parts in slots for piece in parts]
    operands = pieces + [w_keyval] + list(carried or ())
    whole = pl.BlockSpec(memory_space=pltpu.VMEM)
    depth = features * len(slots)
    aliases = {} if carried is None else {len(pieces) + 2: 0, len(pieces) + 3: 1}
    return pl.pallas_call(
        functools.partial(sum_kernel, counts, carried is None),
        out_shape=[pltpu.VMEM((heads, rows, pair), jnp.float32), pltpu.VMEM((TILE, features), jnp.float32)],
        grid_spec=pltpu.PrefetchScalarGridSpec(
            num_scalar_prefetch=1,
            grid=(),
            in_specs=anywhere(len(pieces) + 1) + [whole] * (len(operands) - len(pieces) - 1),
            out_specs=[whole] * 2,
            scratch_shapes=block_scratch(counts, rows, features, heads, pair),
        ),
        input_output_aliases=aliases,
        compiler_params=params(STEP_MIB),
        cost_estimate=pl.CostEstimate(
            flops=rows * depth * heads * pair // 2, bytes_accessed=depth * heads * pair // 2, transcendentals=0
        ),
        name="sum_step",
    )(index, *operands)


def attend_kernel(slots, merging, width, index_ref, *refs):
    refs = list(refs)
    pieces = [[refs.pop(0) for _ in range(count)] for count in slots]
    w_ref, sum_in, tile_in, query_ref = [refs.pop(0) for _ in range(4)]
    if merging:
        context_in, top_in, total_in, w_out_ref = [refs.pop(0) for _ in range(4)]
        theirs_ref, mine_ref = refs.pop(0), refs.pop(0)
    else:
        context_out, top_out, total_out = [refs.pop(0) for _ in range(3)]
    rows_at, tiles, weights, rows_sem, tiles_sem, weights_sem = [refs.pop(0) for _ in range(6)]
    heads, rows, pair = sum_in.shape
    size = pair // 2
    row_copies, tile_copies, weight_copies = start_blocks(
        index_ref, len(slots), pieces, w_ref, rows_at, tiles, weights, rows_sem, tiles_sem, weights_sem
    )
    start_all(row_copies)
    start_all(tile_copies)
    for head in range(heads):
        start_all(weight_copies[head])
    if merging:
        w_out_at, out_sem, merged = refs
        out_copies = [
            pltpu.make_async_copy(w_out_ref.at[head], w_out_at.at[head], out_sem.at[head]) for head in range(heads)
        ]
        start_all(out_copies)
    wait_all(tile_copies)
    squares = sum((tiles[slot].astype(jnp.float32) for slot in range(len(slots))), tile_in[...])
    inverse = lax.rsqrt(lane_sums(squares, rows) / width + epsilon)
    wait_all(row_copies)
    for copies in weight_copies:
        wait_all(copies)
    for head in range(heads):
        keyvals = (
            sum_in[head] + jnp.dot(rows_at[...], weights[head], preferred_element_type=jnp.float32)
        ).astype(jnp.bfloat16)
        scores = inverse * lax.dot_general(
            query_ref[head], keyvals[:, :size], (((1,), (1,)), ((), ())), preferred_element_type=jnp.float32
        )
        top = jnp.max(scores, axis=1, keepdims=True)
        weight = jnp.exp(scores - top)
        norm = jnp.sum(weight, axis=1, keepdims=True)
        context = jnp.dot(
            (weight * inverse).astype(jnp.bfloat16), keyvals[:, size:], preferred_element_type=jnp.float32
        )
        if not merging:
            context_out[head] = context
            top_out[head] = jnp.broadcast_to(top, top_out.shape[1:])
            total_out[head] = jnp.broadcast_to(norm, total_out.shape[1:])
            continue
        other_top, other_norm = top_in[head][:, :1], total_in[head][:, :1]
        highest = jnp.maximum(top, other_top)
        left, right = jnp.exp(top - highest), jnp.exp(other_top - highest)
        whole = left * norm + right * other_norm
        joined = context * (left / whole) + context_in[head] * (right / whole)
        merged[:, head * size : (head + 1) * size] = joined.astype(jnp.bfloat16)
    if not merging:
        return
    wait_all(out_copies)
    count, _, cols = mine_ref.shape
    for part, target in enumerate((theirs_ref, mine_ref)):
        @pl.loop(0, count, unroll=min(count, 4))
        def _(step):
            block = index_ref[len(slots) + part * count + step]
            columns = pl.ds(pl.multiple_of(block * cols, cols), cols)
            out_part = w_out_at[:, :, columns].reshape(heads * size, cols)
            value = jnp.dot(merged[...], out_part, preferred_element_type=jnp.float32)
            target[step] = value.astype(target.dtype)


def attend(index, slots, w_keyval, carried, queries, other=None, w_out=None, blocks=0, cols=0):
    heads, width, pair = w_keyval.shape
    rows = carried[0].shape[1]
    features = slots[0][0].shape[1]
    counts = tuple(len(parts) for parts in slots)
    target, size = queries.shape[1:]
    pieces = [piece for parts in slots for piece in parts]
    operands = pieces + [w_keyval, *carried, queries]
    whole = pl.BlockSpec(memory_space=pltpu.VMEM)
    in_specs = anywhere(len(pieces) + 1) + [whole] * 3
    depth = features * len(slots)
    scratch = block_scratch(counts, rows, features, heads, pair)
    merging = other is not None
    if merging:
        operands += list(other) + [w_out]
        in_specs += [whole] * 3 + anywhere(1)
        scratch += [
            pltpu.VMEM(w_out.shape, w_out.dtype),
            pltpu.SemaphoreType.DMA((heads,)),
            pltpu.VMEM((target, heads * size), jnp.bfloat16),
        ]
        out_shape = [
            jax.ShapeDtypeStruct((blocks, target, cols), jnp.bfloat16),
            pltpu.VMEM((blocks, target, cols), jnp.float32),
        ]
    else:
        out_shape = [pltpu.VMEM((heads, target, last), jnp.float32) for last in (size, 128, 128)]
    return pl.pallas_call(
        functools.partial(attend_kernel, counts, merging, width),
        out_shape=out_shape,
        grid_spec=pltpu.PrefetchScalarGridSpec(
            num_scalar_prefetch=1,
            grid=(),
            in_specs=in_specs,
            out_specs=[whole] * len(out_shape),
            scratch_shapes=scratch,
        ),
        compiler_params=params(STEP_MIB),
        cost_estimate=pl.CostEstimate(
            flops=rows * depth * heads * pair // 2, bytes_accessed=depth * heads * pair // 2, transcendentals=0
        ),
        name="attend",
    )(index, *operands)


def split_kernel(mine_ref, other_ref, keep_ref, *sends):
    lines, rows = keep_ref.shape[0], keep_ref.shape[1]
    part = rows // len(sends)
    for line in range(lines):
        keep_ref[line] = mine_ref[2 * line] + other_ref[2 * line].astype(jnp.float32)
        total = mine_ref[2 * line + 1] + other_ref[2 * line + 1].astype(jnp.float32)
        for which, send in enumerate(sends):
            send[line] = total[which * part : (which + 1) * part].astype(send.dtype)


def split_blocks(mine, other, parts):
    count, target, cols = mine.shape
    sends = [jax.ShapeDtypeStruct((count // 2, target // parts, cols), jnp.bfloat16)] * parts
    return pl.pallas_call(
        split_kernel,
        out_shape=[pltpu.VMEM((count // 2, target, cols), jnp.float32)] + sends,
        compiler_params=params(SMALL_MIB),
        name="split_blocks",
    )(mine, other)


def fold_kernel(which, keep_ref, other_ref, *outs):
    part = other_ref.shape[1]
    for line, out in enumerate(outs):
        kept = keep_ref[line, which * part : (which + 1) * part, :]
        out[...] = (kept + other_ref[line].astype(jnp.float32)).astype(out.dtype)


def fold_blocks(which, keep, other):
    lines, part, cols = other.shape
    return pl.pallas_call(
        functools.partial(fold_kernel, which),
        out_shape=[
            jax.ShapeDtypeStruct((part, cols), jnp.float32 if line == 0 else jnp.bfloat16) for line in range(lines)
        ],
        compiler_params=params(SMALL_MIB),
        name="fold_blocks",
    )(keep, other)


def finish_kernel(lines, index_ref, share_ref, *refs):
    *terms, out_ref = refs
    at = 0
    for first in range(0, len(terms), lines):
        part = terms[first].shape[0]
        total = share_ref[at : at + part, :].astype(jnp.float32)
        for term in terms[first : first + lines]:
            total = total + term[...].astype(jnp.float32)
        out_ref[at : at + part, :] = total.astype(out_ref.dtype)
        at += part


def finish(position, dec_input, parts):
    cols = parts[0][0].shape[1]
    target = dec_input.shape[0]
    terms = [term for part in parts for term in part]
    block = pl.BlockSpec((target, cols), lambda g, i: (0, i[0]))
    return pl.pallas_call(
        functools.partial(finish_kernel, len(parts[0])),
        out_shape=jax.ShapeDtypeStruct((target, cols), jnp.bfloat16),
        grid_spec=pltpu.PrefetchScalarGridSpec(
            num_scalar_prefetch=1,
            grid=(1,),
            in_specs=[block] + [pl.BlockSpec(memory_space=pltpu.VMEM)] * len(terms),
            out_specs=pl.BlockSpec((target, cols), lambda g, i: (0, 0)),
        ),
        compiler_params=params(SMALL_MIB),
        name="finish",
    )(position[None], dec_input, *terms)


def ring_body(enc_rows, enc_gain, dec_input, dec_gain, w_query, w_keyval, w_out):
    sections = lax.axis_size("section")
    position = lax.axis_index("section")
    chips = sections // 2
    ring = ring_order(chips)
    place = {chip: k for k, chip in enumerate(ring)}
    width = dec_input.shape[1]
    cols = width // sections
    head_size = w_query.shape[2]
    score_scale = 1.0 / math.sqrt(head_size)
    far = chips // 2

    def at(chip, offset):
        return ring[(place[chip] + offset) % chips]

    def hop(values, offset):
        pairs = [(2 * chip + core, 2 * at(chip, offset) + core) for chip in range(chips) for core in range(2)]
        return lax.ppermute(values, "section", pairs)

    def exchange(values, bits):
        return lax.ppermute(values, "section", [(s, s ^ bits) for s in range(sections)])

    def swap(values):
        return exchange(values, 1)

    table = []
    for s in range(sections):
        chip, core = divmod(s, 2)
        row = [s, s ^ 1]
        for step in range(1, far):
            for side in (core, 1 - core):
                row += [2 * at(chip, -step) + side, 2 * at(chip, step) + side]
        row += [2 * at(chip, far) + core, 2 * at(chip, far) + 1 - core]
        for side in (1 - core, core):
            row += [2 * (chip ^ k) + side for k in range(chips)]
        table.append(row)
    row = lax.dynamic_slice_in_dim(jnp.asarray(np.array(table, np.int32)), position, 1, 0)[0]
    first_slot = [0] + [2 + 4 * step for step in range(far)]

    half_rows = enc_rows.shape[0] // 2
    state = dec_input.astype(jnp.float32)
    normed = rms_scaled(state, dec_gain[0]).astype(jnp.bfloat16)
    queries = (
        jnp.einsum("td,hdk->htk", normed, w_query, preferred_element_type=jnp.float32) * score_scale
    ).astype(jnp.bfloat16)

    own = [prepare(position, enc_rows, enc_gain, 0)]
    own.append(prepare(position, enc_rows, enc_gain, 1, [queries]))

    carried = [None, None]
    slots = [[(half,), (swap(half),)] for half in own]
    held = [(half, half) for half in own]
    flying = [(hop(half, 1), hop(half, -1)) for half in own]
    token = queries
    for phase in range(2 * far):
        step, which = phase // 2 + 1, phase % 2
        *arrived, token = lax.optimization_barrier((*flying[phase], token))
        if step + 1 < far:
            flying.append((hop(arrived[0], 1), hop(arrived[1], -1)))
        elif step + 1 == far:
            cut = half_rows // 2
            flying.append((hop(arrived[0][:cut], 1), hop(arrived[1][cut:], -1)))
        other = [swap(part) for part in arrived]
        if step < far:
            received = [(part,) for part in arrived + other]
        else:
            received = [tuple(arrived), tuple(other)]
        slots.append(received)
        if phase == 0:
            todo, half, begin = slots[0], 0, 0
        elif phase == 2:
            todo, half, begin = slots[1] + slots[3], 1, 0
        else:
            todo, half, begin = slots[phase + 1], 1 - which, first_slot[(phase + 1) // 2]
        if phase < 2 * far - 1:
            carried[half] = sum_step(row[begin : begin + len(todo)], todo, w_keyval, half_rows, carried[half])
            token = carried[half][1]
    last = first_slot[far]
    first = attend(row[last : last + 2], slots[2 * far], w_keyval, carried[0], queries)
    theirs, mine = attend(row[last:], slots[2 * far + 1], w_keyval, carried[1], queries, first, w_out, chips, cols)
    keep, *sends = split_blocks(mine, swap(theirs), PARTS)
    sends = [exchange(send, 2) for send in sends]
    parts = []
    for which, send in enumerate(sends):
        first, *others = fold_blocks(which, keep, send)
        parts.append([first] + [exchange(term, 4 * (line + 1)) for line, term in enumerate(others)])
    return finish(position, dec_input, parts)


def general_body(enc_rows, enc_gain, dec_input, dec_gain, w_query, w_keyval, w_out):
    sections = lax.axis_size("section")
    position = lax.axis_index("section")
    layers = dec_gain.shape[0]
    target_rows = dec_input.shape[0]
    model_width = dec_input.shape[1]
    head_size = w_query.shape[2]
    score_scale = 1.0 / math.sqrt(head_size)
    my_layer = position // (sections // layers)
    whole_rows = lax.all_gather(enc_rows, "section", axis=1, tiled=True)
    encoded = rms_scaled(whole_rows.astype(jnp.float32), enc_gain).astype(jnp.bfloat16)
    keyvals = jnp.einsum(
        "rd,hdk->rhk", encoded, w_keyval, preferred_element_type=jnp.float32
    ).astype(jnp.bfloat16)
    key_rows = keyvals[:, :, :head_size]
    value_rows = keyvals[:, :, head_size:]

    def head_context(normed):
        queries = (
            jnp.einsum("td,hdk->htk", normed, w_query, preferred_element_type=jnp.float32)
            * score_scale
        ).astype(jnp.bfloat16)
        scores = jnp.einsum("htk,rhk->htr", queries, key_rows, preferred_element_type=jnp.float32)
        weights_bf = jax.nn.softmax(scores, axis=-1).astype(jnp.bfloat16)
        return jnp.einsum(
            "htr,rhk->htk", weights_bf, value_rows, preferred_element_type=jnp.float32
        ).astype(jnp.bfloat16)

    col_share = model_width // sections
    col_start = position * col_share
    state_share = lax.dynamic_slice_in_dim(dec_input, col_start, col_share, 1).astype(jnp.float32)
    for layer_idx in range(layers):
        squares = lax.psum(jnp.sum(state_share * state_share, axis=1), "section")
        gain_share = lax.dynamic_slice_in_dim(dec_gain[layer_idx], col_start, col_share, 0)
        inverse = lax.rsqrt(squares / model_width + epsilon)
        normed_share = (state_share * inverse[:, None] * gain_share).astype(jnp.bfloat16)
        normed = lax.all_gather(normed_share, "section", axis=1, tiled=True)

        def project_out(normed_in):
            return jnp.einsum(
                "htk,hkd->td", head_context(normed_in), w_out, preferred_element_type=jnp.float32
            )

        def skipped(normed_in):
            return jnp.zeros((target_rows, model_width), jnp.float32)

        state_share = state_share + lax.psum_scatter(
            lax.cond(my_layer == layer_idx, project_out, skipped, normed),
            "section",
            scatter_dimension=1,
            tiled=True,
        )
    return state_share.astype(jnp.bfloat16)


def body(enc_rows, enc_gain, dec_input, dec_gain, w_query, w_keyval, w_out):
    chips, odd = divmod(lax.axis_size("section"), 2)
    ringed = not odd and 4 <= chips <= MAX_RING and chips & (chips - 1) == 0 and dec_gain.shape[0] == 1
    chosen = ring_body if ringed else general_body
    return chosen(enc_rows, enc_gain, dec_input, dec_gain, w_query, w_keyval, w_out)


def solution(mesh):
    in_specs = (
        P("groups", "section"),
        P(),
        P("groups", None),
        P(),
        P("section", None, None),
        P("section", None, None),
        P("section", None, None),
    )
    out_specs = P("groups", "section")
    return jax.shard_map(body, mesh=mesh, in_specs=in_specs, out_specs=out_specs, check_vma=False)
```

```python
import functools
import math

import jax
import jax.numpy as jnp
import numpy as np
from jax import lax
from jax.experimental import pallas as pl
from jax.experimental.pallas import tpu as pltpu
from jax.sharding import PartitionSpec as P

epsilon = 1e-06
MAX_RING = 8
SMALL_MIB = 16
PARTS = 2
STEP_MIB = 20
TILE = 16


def rms_scaled(values, gain):
    return values * lax.rsqrt(jnp.mean(values * values, axis=-1, keepdims=True) + epsilon) * gain


def ring_order(chips):
    return list(range(0, chips, 2)) + list(range(1, chips, 2))[::-1]


def params(mib):
    return pltpu.CompilerParams(vmem_limit_bytes=mib * 2**20)


def anywhere(count):
    return [pl.BlockSpec(memory_space=pl.ANY)] * count


def prepare_kernel(index_ref, rows_ref, gain_ref, *refs):
    half_ref = refs[-1]
    rows, cols = rows_ref.shape
    values = rows_ref[...].astype(jnp.float32)
    half_ref[:rows, :] = (values * gain_ref[...]).astype(jnp.bfloat16)
    squares = values * values
    high = squares.astype(jnp.bfloat16)
    low = (squares - high.astype(jnp.float32)).astype(jnp.bfloat16)
    ones = jnp.ones((8, cols), jnp.bfloat16)
    sums = sum(
        lax.dot_general(ones, part, (((1,), (1,)), ((), ())), preferred_element_type=jnp.float32)
        for part in (high, low)
    )[:1]
    terms = []
    for _ in range(3):
        terms.append(sums.astype(jnp.bfloat16).astype(jnp.float32))
        sums = sums - terms[-1]
    lines = []
    for term in terms:
        for line in range(-(-rows // cols)):
            part = term[:, line * cols : min(rows, (line + 1) * cols)]
            if part.shape[1] < cols:
                part = jnp.concatenate([part, jnp.zeros((1, cols - part.shape[1]), jnp.float32)], axis=1)
            lines.append(part)
    lines.append(jnp.zeros((TILE - len(lines), cols), jnp.float32))
    half_ref[rows:, :] = jnp.concatenate(lines, axis=0).astype(jnp.bfloat16)


def prepare(position, enc_rows, enc_gain, which, before=()):
    rows, cols = enc_rows.shape[0] // 2, enc_rows.shape[1]
    return pl.pallas_call(
        prepare_kernel,
        out_shape=jax.ShapeDtypeStruct((rows + TILE, cols), jnp.bfloat16),
        grid_spec=pltpu.PrefetchScalarGridSpec(
            num_scalar_prefetch=1,
            grid=(1,),
            in_specs=[
                pl.BlockSpec((rows, cols), lambda g, i: (which, 0)),
                pl.BlockSpec((1, cols), lambda g, i: (0, i[0])),
            ]
            + anywhere(len(before)),
            out_specs=pl.BlockSpec((rows + TILE, cols), lambda g, i: (0, 0)),
        ),
        compiler_params=params(SMALL_MIB),
        name="prepare",
    )(position[None], enc_rows, enc_gain[None, :], *before)


def lane_sums(tile, rows):
    cols = tile.shape[1]
    per = -(-rows // cols)
    lines = []
    for line in range(per):
        term = sum(tile[k * per + line : k * per + line + 1, :] for k in range(3))
        lines.append(term[:, : min(cols, rows - line * cols)])
    return jnp.concatenate(lines, axis=1)


def slot_weights(index_ref, w_ref, head, slot, features):
    return w_ref[head, pl.ds(pl.multiple_of(index_ref[slot] * features, features), features), :]


def slot_squares(arrays, slots):
    ends = [(which, at + length) for which, at, length in (parts[-1] for parts in slots)]
    return sum(arrays[which][end : end + TILE, :].astype(jnp.float32) for which, end in ends)


def gather_slots(slots):
    arrays, placed = [], []
    for parts in slots:
        line = []
        for array, at, length in parts:
            found = [k for k, known in enumerate(arrays) if known is array]
            if not found:
                arrays.append(array)
            line.append((found[0] if found else len(arrays) - 1, at, length))
        placed.append(tuple(line))
    return arrays, tuple(placed)


def sum_kernel(slots, count, first, index_ref, *refs):
    refs = list(refs)
    arrays = [refs.pop(0) for _ in range(count)]
    w_ref = refs.pop(0)
    sum_in, tile_in = (None, None) if first else (refs.pop(0), refs.pop(0))
    sum_out, tile_out = refs
    heads = sum_out.shape[0]
    features = tile_out.shape[1]
    for head in range(heads):
        total = None if first else sum_in[head]
        for slot, ((which, at, length),) in enumerate(slots):
            term = jnp.dot(
                arrays[which][at : at + length, :],
                slot_weights(index_ref, w_ref, head, slot, features),
                preferred_element_type=jnp.float32,
            )
            total = term if total is None else total + term
        sum_out[head] = total
    squares = slot_squares(arrays, slots)
    tile_out[...] = squares if first else tile_in[...] + squares


def sum_step(index, slots, w_keyval, rows, carried=None):
    heads, width, pair = w_keyval.shape
    arrays, placed = gather_slots(slots)
    features = arrays[0].shape[1]
    operands = arrays + [w_keyval] + list(carried or ())
    whole = pl.BlockSpec(memory_space=pltpu.VMEM)
    depth = features * len(slots)
    aliases = {} if carried is None else {len(arrays) + 2: 0, len(arrays) + 3: 1}
    return pl.pallas_call(
        functools.partial(sum_kernel, placed, len(arrays), carried is None),
        out_shape=[pltpu.VMEM((heads, rows, pair), jnp.float32), pltpu.VMEM((TILE, features), jnp.float32)],
        grid_spec=pltpu.PrefetchScalarGridSpec(
            num_scalar_prefetch=1, grid=(), in_specs=[whole] * len(operands), out_specs=[whole] * 2
        ),
        input_output_aliases=aliases,
        compiler_params=params(STEP_MIB),
        cost_estimate=pl.CostEstimate(
            flops=rows * depth * heads * pair // 2, bytes_accessed=depth * heads * pair // 2, transcendentals=0
        ),
        name="sum_step",
    )(index, *operands)


def attend_kernel(slots, count, merging, width, index_ref, *refs):
    refs = list(refs)
    arrays = [refs.pop(0) for _ in range(count)]
    w_ref, sum_in, tile_in, query_ref = [refs.pop(0) for _ in range(4)]
    if merging:
        context_in, top_in, total_in, w_out_ref, theirs_ref, mine_ref, w_out_at, out_sem, merged = refs
        out_copies = [
            pltpu.make_async_copy(w_out_ref.at[head], w_out_at.at[head], out_sem.at[head])
            for head in range(w_out_at.shape[0])
        ]
        for copy in out_copies:
            copy.start()
    else:
        context_out, top_out, total_out = refs
    heads, rows, pair = sum_in.shape
    features = tile_in.shape[1]
    size = pair // 2
    squares = tile_in[...] + slot_squares(arrays, slots)
    inverse = lax.rsqrt(lane_sums(squares, rows) / width + epsilon)
    for head in range(heads):
        parts, first = [], 0
        for part in range(len(slots[0])):
            length = slots[0][part][2]
            total = sum_in[head, first : first + length, :]
            for slot in range(len(slots)):
                which, at, _ = slots[slot][part]
                total = total + jnp.dot(
                    arrays[which][at : at + length, :],
                    slot_weights(index_ref, w_ref, head, slot, features),
                    preferred_element_type=jnp.float32,
                )
            parts.append(total.astype(jnp.bfloat16))
            first += length
        keyvals = jnp.concatenate(parts, axis=0)
        scores = inverse * lax.dot_general(
            query_ref[head], keyvals[:, :size], (((1,), (1,)), ((), ())), preferred_element_type=jnp.float32
        )
        top = jnp.max(scores, axis=1, keepdims=True)
        weight = jnp.exp(scores - top)
        norm = jnp.sum(weight, axis=1, keepdims=True)
        context = jnp.dot(
            (weight * inverse).astype(jnp.bfloat16), keyvals[:, size:], preferred_element_type=jnp.float32
        )
        if not merging:
            context_out[head] = context
            top_out[head] = jnp.broadcast_to(top, top_out.shape[1:])
            total_out[head] = jnp.broadcast_to(norm, total_out.shape[1:])
            continue
        other_top, other_norm = top_in[head][:, :1], total_in[head][:, :1]
        highest = jnp.maximum(top, other_top)
        left, right = jnp.exp(top - highest), jnp.exp(other_top - highest)
        whole = left * norm + right * other_norm
        joined = context * (left / whole) + context_in[head] * (right / whole)
        merged[:, head * size : (head + 1) * size] = joined.astype(jnp.bfloat16)
    if not merging:
        return
    for copy in out_copies:
        copy.wait()
    count, _, cols = mine_ref.shape
    for part, target in enumerate((theirs_ref, mine_ref)):
        @pl.loop(0, count, unroll=min(count, 4))
        def _(step):
            block = index_ref[len(slots) + part * count + step]
            columns = pl.ds(pl.multiple_of(block * cols, cols), cols)
            out_part = w_out_at[:, :, columns].reshape(heads * size, cols)
            value = jnp.dot(merged[...], out_part, preferred_element_type=jnp.float32)
            target[step] = value.astype(target.dtype)


def attend(index, slots, w_keyval, carried, queries, other=None, w_out=None, blocks=0, cols=0):
    heads, width, pair = w_keyval.shape
    rows = carried[0].shape[1]
    arrays, placed = gather_slots(slots)
    features = arrays[0].shape[1]
    target, size = queries.shape[1:]
    operands = arrays + [w_keyval, *carried, queries]
    whole = pl.BlockSpec(memory_space=pltpu.VMEM)
    depth = features * len(slots)
    merging = other is not None
    in_specs, scratch = [whole] * len(operands), []
    if merging:
        operands += list(other) + [w_out]
        in_specs += [whole] * 3 + anywhere(1)
        scratch = [
            pltpu.VMEM(w_out.shape, w_out.dtype),
            pltpu.SemaphoreType.DMA((heads,)),
            pltpu.VMEM((target, heads * size), jnp.bfloat16),
        ]
        out_shape = [
            jax.ShapeDtypeStruct((blocks, target, cols), jnp.bfloat16),
            pltpu.VMEM((blocks, target, cols), jnp.float32),
        ]
    else:
        out_shape = [pltpu.VMEM((heads, target, last), jnp.float32) for last in (size, 128, 128)]
    return pl.pallas_call(
        functools.partial(attend_kernel, placed, len(arrays), merging, width),
        out_shape=out_shape,
        grid_spec=pltpu.PrefetchScalarGridSpec(
            num_scalar_prefetch=1,
            grid=(),
            in_specs=in_specs,
            out_specs=[whole] * len(out_shape),
            scratch_shapes=scratch,
        ),
        compiler_params=params(STEP_MIB),
        cost_estimate=pl.CostEstimate(
            flops=rows * depth * heads * pair // 2, bytes_accessed=depth * heads * pair // 2, transcendentals=0
        ),
        name="attend",
    )(index, *operands)


def split_kernel(mine_ref, other_ref, keep_ref, *sends):
    lines, rows = keep_ref.shape[0], keep_ref.shape[1]
    part = rows // len(sends)
    for line in range(lines):
        keep_ref[line] = mine_ref[2 * line] + other_ref[2 * line].astype(jnp.float32)
        total = mine_ref[2 * line + 1] + other_ref[2 * line + 1].astype(jnp.float32)
        for which, send in enumerate(sends):
            send[line] = total[which * part : (which + 1) * part].astype(send.dtype)


def split_blocks(mine, other, parts):
    count, target, cols = mine.shape
    sends = [jax.ShapeDtypeStruct((count // 2, target // parts, cols), jnp.bfloat16)] * parts
    return pl.pallas_call(
        split_kernel,
        out_shape=[pltpu.VMEM((count // 2, target, cols), jnp.float32)] + sends,
        compiler_params=params(SMALL_MIB),
        name="split_blocks",
    )(mine, other)


def fold_kernel(which, keep_ref, other_ref, *outs):
    part = other_ref.shape[1]
    for line, out in enumerate(outs):
        kept = keep_ref[line, which * part : (which + 1) * part, :]
        out[...] = (kept + other_ref[line].astype(jnp.float32)).astype(out.dtype)


def fold_blocks(which, keep, other):
    lines, part, cols = other.shape
    return pl.pallas_call(
        functools.partial(fold_kernel, which),
        out_shape=[
            jax.ShapeDtypeStruct((part, cols), jnp.float32 if line == 0 else jnp.bfloat16) for line in range(lines)
        ],
        compiler_params=params(SMALL_MIB),
        name="fold_blocks",
    )(keep, other)


def finish_kernel(lines, index_ref, share_ref, *refs):
    *terms, out_ref = refs
    at = 0
    for first in range(0, len(terms), lines):
        part = terms[first].shape[0]
        total = share_ref[at : at + part, :].astype(jnp.float32)
        for term in terms[first : first + lines]:
            total = total + term[...].astype(jnp.float32)
        out_ref[at : at + part, :] = total.astype(out_ref.dtype)
        at += part


def finish(position, dec_input, parts):
    cols = parts[0][0].shape[1]
    target = dec_input.shape[0]
    terms = [term for part in parts for term in part]
    block = pl.BlockSpec((target, cols), lambda g, i: (0, i[0]))
    return pl.pallas_call(
        functools.partial(finish_kernel, len(parts[0])),
        out_shape=jax.ShapeDtypeStruct((target, cols), jnp.bfloat16),
        grid_spec=pltpu.PrefetchScalarGridSpec(
            num_scalar_prefetch=1,
            grid=(1,),
            in_specs=[block] + [pl.BlockSpec(memory_space=pltpu.VMEM)] * len(terms),
            out_specs=pl.BlockSpec((target, cols), lambda g, i: (0, 0)),
        ),
        compiler_params=params(SMALL_MIB),
        name="finish",
    )(position[None], dec_input, *terms)


def ring_body(enc_rows, enc_gain, dec_input, dec_gain, w_query, w_keyval, w_out):
    sections = lax.axis_size("section")
    position = lax.axis_index("section")
    chips = sections // 2
    ring = ring_order(chips)
    place = {chip: k for k, chip in enumerate(ring)}
    width = dec_input.shape[1]
    cols = width // sections
    head_size = w_query.shape[2]
    score_scale = 1.0 / math.sqrt(head_size)
    far = chips // 2

    def at(chip, offset):
        return ring[(place[chip] + offset) % chips]

    def hop(values, offset):
        pairs = [(2 * chip + core, 2 * at(chip, offset) + core) for chip in range(chips) for core in range(2)]
        return lax.ppermute(values, "section", pairs)

    def exchange(values, bits):
        return lax.ppermute(values, "section", [(s, s ^ bits) for s in range(sections)])

    def swap(values):
        return exchange(values, 1)

    table = []
    for s in range(sections):
        chip, core = divmod(s, 2)
        row = [s, s ^ 1]
        for step in range(1, far):
            for side in (core, 1 - core):
                row += [2 * at(chip, -step) + side, 2 * at(chip, step) + side]
        row += [2 * at(chip, far) + core, 2 * at(chip, far) + 1 - core]
        for side in (1 - core, core):
            row += [2 * (chip ^ k) + side for k in range(chips)]
        table.append(row)
    row = lax.dynamic_slice_in_dim(jnp.asarray(np.array(table, np.int32)), position, 1, 0)[0]
    first_slot = [0] + [2 + 4 * step for step in range(far)]

    half_rows = enc_rows.shape[0] // 2
    state = dec_input.astype(jnp.float32)
    normed = rms_scaled(state, dec_gain[0]).astype(jnp.bfloat16)
    queries = (
        jnp.einsum("td,hdk->htk", normed, w_query, preferred_element_type=jnp.float32) * score_scale
    ).astype(jnp.bfloat16)

    own = [prepare(position, enc_rows, enc_gain, 0)]
    own.append(prepare(position, enc_rows, enc_gain, 1, [queries, row]))

    carried = [None, None]
    slots = [[[(half, 0, half_rows)], [(swap(half), 0, half_rows)]] for half in own]
    held = [(half, half) for half in own]
    flying = [(hop(half, 1), hop(half, -1)) for half in own]
    token = own[1]
    for phase in range(2 * far):
        step, which = phase // 2 + 1, phase % 2
        *arrived, token = lax.optimization_barrier((*flying[phase], token))
        if step + 1 < far:
            flying.append((hop(arrived[0], 1), hop(arrived[1], -1)))
        elif step + 1 == far:
            cut = half_rows // 2
            flying.append((hop(arrived[0][:cut], 1), hop(arrived[1][cut:], -1)))
        other = swap(jnp.concatenate(arrived, axis=0))
        length = arrived[0].shape[0]
        if step < far:
            received = [[(part, 0, half_rows)] for part in arrived]
            received += [[(other, at, half_rows)] for at in (0, length)]
        else:
            rest = half_rows - length
            received = [
                [(arrived[0], 0, length), (arrived[1], 0, rest)],
                [(other, 0, length), (other, length, rest)],
            ]
        slots.append(received)
        if phase == 0:
            todo, half, begin = slots[0], 0, 0
        elif phase == 2:
            todo, half, begin = slots[1] + slots[3], 1, 0
        else:
            todo, half, begin = slots[phase + 1], 1 - which, first_slot[(phase + 1) // 2]
        if phase < 2 * far - 1:
            carried[half] = sum_step(row[begin : begin + len(todo)], todo, w_keyval, half_rows, carried[half])
            token = carried[half][1]
    last = first_slot[far]
    first = attend(row[last : last + 2], slots[2 * far], w_keyval, carried[0], queries)
    theirs, mine = attend(row[last:], slots[2 * far + 1], w_keyval, carried[1], queries, first, w_out, chips, cols)
    keep, *sends = split_blocks(mine, swap(theirs), PARTS)
    sends = [exchange(send, 2) for send in sends]
    parts = []
    for which, send in enumerate(sends):
        first, *others = fold_blocks(which, keep, send)
        lines = [*range(1, len(others)), 0]
        parts.append([first] + [exchange(others[line], 4 * (line + 1)) for line in lines])
    return finish(position, dec_input, parts)


def general_body(enc_rows, enc_gain, dec_input, dec_gain, w_query, w_keyval, w_out):
    sections = lax.axis_size("section")
    position = lax.axis_index("section")
    layers = dec_gain.shape[0]
    target_rows = dec_input.shape[0]
    model_width = dec_input.shape[1]
    head_size = w_query.shape[2]
    score_scale = 1.0 / math.sqrt(head_size)
    my_layer = position // (sections // layers)
    whole_rows = lax.all_gather(enc_rows, "section", axis=1, tiled=True)
    encoded = rms_scaled(whole_rows.astype(jnp.float32), enc_gain).astype(jnp.bfloat16)
    keyvals = jnp.einsum(
        "rd,hdk->rhk", encoded, w_keyval, preferred_element_type=jnp.float32
    ).astype(jnp.bfloat16)
    key_rows = keyvals[:, :, :head_size]
    value_rows = keyvals[:, :, head_size:]

    def head_context(normed):
        queries = (
            jnp.einsum("td,hdk->htk", normed, w_query, preferred_element_type=jnp.float32)
            * score_scale
        ).astype(jnp.bfloat16)
        scores = jnp.einsum("htk,rhk->htr", queries, key_rows, preferred_element_type=jnp.float32)
        weights_bf = jax.nn.softmax(scores, axis=-1).astype(jnp.bfloat16)
        return jnp.einsum(
            "htr,rhk->htk", weights_bf, value_rows, preferred_element_type=jnp.float32
        ).astype(jnp.bfloat16)

    col_share = model_width // sections
    col_start = position * col_share
    state_share = lax.dynamic_slice_in_dim(dec_input, col_start, col_share, 1).astype(jnp.float32)
    for layer_idx in range(layers):
        squares = lax.psum(jnp.sum(state_share * state_share, axis=1), "section")
        gain_share = lax.dynamic_slice_in_dim(dec_gain[layer_idx], col_start, col_share, 0)
        inverse = lax.rsqrt(squares / model_width + epsilon)
        normed_share = (state_share * inverse[:, None] * gain_share).astype(jnp.bfloat16)
        normed = lax.all_gather(normed_share, "section", axis=1, tiled=True)

        def project_out(normed_in):
            return jnp.einsum(
                "htk,hkd->td", head_context(normed_in), w_out, preferred_element_type=jnp.float32
            )

        def skipped(normed_in):
            return jnp.zeros((target_rows, model_width), jnp.float32)

        state_share = state_share + lax.psum_scatter(
            lax.cond(my_layer == layer_idx, project_out, skipped, normed),
            "section",
            scatter_dimension=1,
            tiled=True,
        )
    return state_share.astype(jnp.bfloat16)


def body(enc_rows, enc_gain, dec_input, dec_gain, w_query, w_keyval, w_out):
    chips, odd = divmod(lax.axis_size("section"), 2)
    ringed = not odd and 4 <= chips <= MAX_RING and chips & (chips - 1) == 0 and dec_gain.shape[0] == 1
    chosen = ring_body if ringed else general_body
    return chosen(enc_rows, enc_gain, dec_input, dec_gain, w_query, w_keyval, w_out)


def solution(mesh):
    in_specs = (
        P("groups", "section"),
        P(),
        P("groups", None),
        P(),
        P("section", None, None),
        P("section", None, None),
        P("section", None, None),
    )
    out_specs = P("groups", "section")
    return jax.shard_map(body, mesh=mesh, in_specs=in_specs, out_specs=out_specs, check_vma=False)
```

```python
import functools
import math

import jax
import jax.numpy as jnp
import numpy as np
from jax import lax
from jax.experimental import pallas as pl
from jax.experimental.pallas import tpu as pltpu
from jax.sharding import PartitionSpec as P

epsilon = 1e-06
MAX_RING = 8
SMALL_MIB = 16
PARTS = 2
STEP_MIB = 20
TILE = 16


def rms_scaled(values, gain):
    return values * lax.rsqrt(jnp.mean(values * values, axis=-1, keepdims=True) + epsilon) * gain


def ring_order(chips):
    return list(range(0, chips, 2)) + list(range(1, chips, 2))[::-1]


def params(mib):
    return pltpu.CompilerParams(vmem_limit_bytes=mib * 2**20)


def anywhere(count):
    return [pl.BlockSpec(memory_space=pl.ANY)] * count


def prepare_kernel(index_ref, rows_ref, gain_ref, *refs):
    half_ref = refs[-1]
    rows, cols = rows_ref.shape
    values = rows_ref[...].astype(jnp.float32)
    half_ref[:rows, :] = (values * gain_ref[...]).astype(jnp.bfloat16)
    squares = values * values
    high = squares.astype(jnp.bfloat16)
    low = (squares - high.astype(jnp.float32)).astype(jnp.bfloat16)
    ones = jnp.ones((8, cols), jnp.bfloat16)
    sums = sum(
        lax.dot_general(ones, part, (((1,), (1,)), ((), ())), preferred_element_type=jnp.float32)
        for part in (high, low)
    )[:1]
    terms = []
    for _ in range(3):
        terms.append(sums.astype(jnp.bfloat16).astype(jnp.float32))
        sums = sums - terms[-1]
    lines = []
    for term in terms:
        for line in range(-(-rows // cols)):
            part = term[:, line * cols : min(rows, (line + 1) * cols)]
            if part.shape[1] < cols:
                part = jnp.concatenate([part, jnp.zeros((1, cols - part.shape[1]), jnp.float32)], axis=1)
            lines.append(part)
    lines.append(jnp.zeros((TILE - len(lines), cols), jnp.float32))
    half_ref[rows:, :] = jnp.concatenate(lines, axis=0).astype(jnp.bfloat16)


def prepare(position, enc_rows, enc_gain, which, before=()):
    rows, cols = enc_rows.shape[0] // 2, enc_rows.shape[1]
    return pl.pallas_call(
        prepare_kernel,
        out_shape=jax.ShapeDtypeStruct((rows + TILE, cols), jnp.bfloat16),
        grid_spec=pltpu.PrefetchScalarGridSpec(
            num_scalar_prefetch=1,
            grid=(1,),
            in_specs=[
                pl.BlockSpec((rows, cols), lambda g, i: (which, 0)),
                pl.BlockSpec((1, cols), lambda g, i: (0, i[0])),
            ]
            + anywhere(len(before)),
            out_specs=pl.BlockSpec((rows + TILE, cols), lambda g, i: (0, 0)),
        ),
        compiler_params=params(SMALL_MIB),
        name="prepare",
    )(position[None], enc_rows, enc_gain[None, :], *before)


def lane_sums(tile, rows):
    cols = tile.shape[1]
    per = -(-rows // cols)
    lines = []
    for line in range(per):
        term = sum(tile[k * per + line : k * per + line + 1, :] for k in range(3))
        lines.append(term[:, : min(cols, rows - line * cols)])
    return jnp.concatenate(lines, axis=1)


def slot_weights(index_ref, w_ref, head, slot, features):
    return w_ref[head, pl.ds(pl.multiple_of(index_ref[slot] * features, features), features), :]


def slot_squares(arrays, slots):
    ends = [(which, at + length) for which, at, length in (parts[-1] for parts in slots)]
    return sum(arrays[which][end : end + TILE, :].astype(jnp.float32) for which, end in ends)


def gather_slots(slots):
    arrays, placed = [], []
    for parts in slots:
        line = []
        for array, at, length in parts:
            found = [k for k, known in enumerate(arrays) if known is array]
            if not found:
                arrays.append(array)
            line.append((found[0] if found else len(arrays) - 1, at, length))
        placed.append(tuple(line))
    return arrays, tuple(placed)


def sum_kernel(slots, count, first, index_ref, *refs):
    refs = list(refs)
    arrays = [refs.pop(0) for _ in range(count)]
    w_ref = refs.pop(0)
    sum_in, tile_in = (None, None) if first else (refs.pop(0), refs.pop(0))
    sum_out, tile_out = refs
    heads = sum_out.shape[0]
    features = tile_out.shape[1]
    for head in range(heads):
        total = None if first else sum_in[head]
        for slot, ((which, at, length),) in enumerate(slots):
            term = jnp.dot(
                arrays[which][at : at + length, :],
                slot_weights(index_ref, w_ref, head, slot, features),
                preferred_element_type=jnp.float32,
            )
            total = term if total is None else total + term
        sum_out[head] = total
    squares = slot_squares(arrays, slots)
    tile_out[...] = squares if first else tile_in[...] + squares


def sum_step(index, slots, w_keyval, rows, carried=None):
    heads, width, pair = w_keyval.shape
    arrays, placed = gather_slots(slots)
    features = arrays[0].shape[1]
    operands = arrays + [w_keyval] + list(carried or ())
    whole = pl.BlockSpec(memory_space=pltpu.VMEM)
    depth = features * len(slots)
    aliases = {} if carried is None else {len(arrays) + 2: 0, len(arrays) + 3: 1}
    return pl.pallas_call(
        functools.partial(sum_kernel, placed, len(arrays), carried is None),
        out_shape=[pltpu.VMEM((heads, rows, pair), jnp.float32), pltpu.VMEM((TILE, features), jnp.float32)],
        grid_spec=pltpu.PrefetchScalarGridSpec(
            num_scalar_prefetch=1, grid=(), in_specs=[whole] * len(operands), out_specs=[whole] * 2
        ),
        input_output_aliases=aliases,
        compiler_params=params(STEP_MIB),
        cost_estimate=pl.CostEstimate(
            flops=rows * depth * heads * pair // 2, bytes_accessed=depth * heads * pair // 2, transcendentals=0
        ),
        name="sum_step",
    )(index, *operands)


def attend_kernel(slots, count, merging, width, index_ref, *refs):
    refs = list(refs)
    arrays = [refs.pop(0) for _ in range(count)]
    w_ref, sum_in, tile_in, query_ref = [refs.pop(0) for _ in range(4)]
    if merging:
        context_in, top_in, total_in, w_out_ref, theirs_ref, mine_ref, w_out_at, out_sem, merged = refs
        out_copies = [
            pltpu.make_async_copy(w_out_ref.at[head], w_out_at.at[head], out_sem.at[head])
            for head in range(w_out_at.shape[0])
        ]
        for copy in out_copies:
            copy.start()
    else:
        context_out, top_out, total_out = refs
    heads, rows, pair = sum_in.shape
    features = tile_in.shape[1]
    size = pair // 2
    squares = tile_in[...] + slot_squares(arrays, slots)
    inverse = lax.rsqrt(lane_sums(squares, rows) / width + epsilon)
    for head in range(heads):
        parts, first = [], 0
        for part in range(len(slots[0])):
            length = slots[0][part][2]
            total = sum_in[head, first : first + length, :]
            for slot in range(len(slots)):
                which, at, _ = slots[slot][part]
                total = total + jnp.dot(
                    arrays[which][at : at + length, :],
                    slot_weights(index_ref, w_ref, head, slot, features),
                    preferred_element_type=jnp.float32,
                )
            parts.append(total.astype(jnp.bfloat16))
            first += length
        keyvals = jnp.concatenate(parts, axis=0)
        scores = inverse * lax.dot_general(
            query_ref[head], keyvals[:, :size], (((1,), (1,)), ((), ())), preferred_element_type=jnp.float32
        )
        top = jnp.max(scores, axis=1, keepdims=True)
        weight = jnp.exp(scores - top)
        norm = jnp.sum(weight, axis=1, keepdims=True)
        context = jnp.dot(
            (weight * inverse).astype(jnp.bfloat16), keyvals[:, size:], preferred_element_type=jnp.float32
        )
        if not merging:
            context_out[head] = context
            top_out[head] = jnp.broadcast_to(top, top_out.shape[1:])
            total_out[head] = jnp.broadcast_to(norm, total_out.shape[1:])
            continue
        other_top, other_norm = top_in[head][:, :1], total_in[head][:, :1]
        highest = jnp.maximum(top, other_top)
        left, right = jnp.exp(top - highest), jnp.exp(other_top - highest)
        whole = left * norm + right * other_norm
        joined = context * (left / whole) + context_in[head] * (right / whole)
        merged[:, head * size : (head + 1) * size] = joined.astype(jnp.bfloat16)
    if not merging:
        return
    for copy in out_copies:
        copy.wait()
    count, _, cols = mine_ref.shape
    for part, target in enumerate((theirs_ref, mine_ref)):
        @pl.loop(0, count, unroll=min(count, 8))
        def _(step):
            block = index_ref[len(slots) + part * count + step]
            columns = pl.ds(pl.multiple_of(block * cols, cols), cols)
            out_part = w_out_at[:, :, columns].reshape(heads * size, cols)
            value = jnp.dot(merged[...], out_part, preferred_element_type=jnp.float32)
            target[step] = value.astype(target.dtype)


def attend(index, slots, w_keyval, carried, queries, other=None, w_out=None, blocks=0, cols=0):
    heads, width, pair = w_keyval.shape
    rows = carried[0].shape[1]
    arrays, placed = gather_slots(slots)
    features = arrays[0].shape[1]
    target, size = queries.shape[1:]
    operands = arrays + [w_keyval, *carried, queries]
    whole = pl.BlockSpec(memory_space=pltpu.VMEM)
    depth = features * len(slots)
    merging = other is not None
    in_specs, scratch = [whole] * len(operands), []
    if merging:
        operands += list(other) + [w_out]
        in_specs += [whole] * 3 + anywhere(1)
        scratch = [
            pltpu.VMEM(w_out.shape, w_out.dtype),
            pltpu.SemaphoreType.DMA((heads,)),
            pltpu.VMEM((target, heads * size), jnp.bfloat16),
        ]
        out_shape = [
            jax.ShapeDtypeStruct((blocks, target, cols), jnp.bfloat16),
            pltpu.VMEM((blocks, target, cols), jnp.float32),
        ]
    else:
        out_shape = [pltpu.VMEM((heads, target, last), jnp.float32) for last in (size, 128, 128)]
    return pl.pallas_call(
        functools.partial(attend_kernel, placed, len(arrays), merging, width),
        out_shape=out_shape,
        grid_spec=pltpu.PrefetchScalarGridSpec(
            num_scalar_prefetch=1,
            grid=(),
            in_specs=in_specs,
            out_specs=[whole] * len(out_shape),
            scratch_shapes=scratch,
        ),
        compiler_params=params(STEP_MIB),
        cost_estimate=pl.CostEstimate(
            flops=rows * depth * heads * pair // 2, bytes_accessed=depth * heads * pair // 2, transcendentals=0
        ),
        name="attend",
    )(index, *operands)


def split_kernel(mine_ref, other_ref, keep_ref, *sends):
    lines, rows = keep_ref.shape[0], keep_ref.shape[1]
    part = rows // len(sends)
    for line in range(lines):
        keep_ref[line] = mine_ref[2 * line] + other_ref[2 * line].astype(jnp.float32)
        total = mine_ref[2 * line + 1] + other_ref[2 * line + 1].astype(jnp.float32)
        for which, send in enumerate(sends):
            send[line] = total[which * part : (which + 1) * part].astype(send.dtype)


def split_blocks(mine, other, parts):
    count, target, cols = mine.shape
    sends = [jax.ShapeDtypeStruct((count // 2, target // parts, cols), jnp.bfloat16)] * parts
    return pl.pallas_call(
        split_kernel,
        out_shape=[pltpu.VMEM((count // 2, target, cols), jnp.float32)] + sends,
        compiler_params=params(SMALL_MIB),
        name="split_blocks",
    )(mine, other)


def fold_kernel(which, keep_ref, other_ref, *outs):
    part = other_ref.shape[1]
    for line, out in enumerate(outs):
        kept = keep_ref[line, which * part : (which + 1) * part, :]
        out[...] = (kept + other_ref[line].astype(jnp.float32)).astype(out.dtype)


def fold_blocks(which, keep, other):
    lines, part, cols = other.shape
    return pl.pallas_call(
        functools.partial(fold_kernel, which),
        out_shape=[
            jax.ShapeDtypeStruct((part, cols), jnp.float32 if line == 0 else jnp.bfloat16) for line in range(lines)
        ],
        compiler_params=params(SMALL_MIB),
        name="fold_blocks",
    )(keep, other)


def finish_kernel(lines, index_ref, share_ref, *refs):
    *terms, out_ref = refs
    at = 0
    for first in range(0, len(terms), lines):
        part = terms[first].shape[0]
        total = share_ref[at : at + part, :].astype(jnp.float32)
        for term in terms[first : first + lines]:
            total = total + term[...].astype(jnp.float32)
        out_ref[at : at + part, :] = total.astype(out_ref.dtype)
        at += part


def finish(position, dec_input, parts):
    cols = parts[0][0].shape[1]
    target = dec_input.shape[0]
    terms = [term for part in parts for term in part]
    block = pl.BlockSpec((target, cols), lambda g, i: (0, i[0]))
    return pl.pallas_call(
        functools.partial(finish_kernel, len(parts[0])),
        out_shape=jax.ShapeDtypeStruct((target, cols), jnp.bfloat16),
        grid_spec=pltpu.PrefetchScalarGridSpec(
            num_scalar_prefetch=1,
            grid=(1,),
            in_specs=[block] + [pl.BlockSpec(memory_space=pltpu.VMEM)] * len(terms),
            out_specs=pl.BlockSpec((target, cols), lambda g, i: (0, 0)),
        ),
        compiler_params=params(SMALL_MIB),
        name="finish",
    )(position[None], dec_input, *terms)


def ring_body(enc_rows, enc_gain, dec_input, dec_gain, w_query, w_keyval, w_out):
    sections = lax.axis_size("section")
    position = lax.axis_index("section")
    chips = sections // 2
    ring = ring_order(chips)
    place = {chip: k for k, chip in enumerate(ring)}
    width = dec_input.shape[1]
    cols = width // sections
    head_size = w_query.shape[2]
    score_scale = 1.0 / math.sqrt(head_size)
    far = chips // 2

    def at(chip, offset):
        return ring[(place[chip] + offset) % chips]

    def hop(values, offset):
        pairs = [(2 * chip + core, 2 * at(chip, offset) + core) for chip in range(chips) for core in range(2)]
        return lax.ppermute(values, "section", pairs)

    def exchange(values, bits):
        return lax.ppermute(values, "section", [(s, s ^ bits) for s in range(sections)])

    def swap(values):
        return exchange(values, 1)

    table = []
    for s in range(sections):
        chip, core = divmod(s, 2)
        row = [s, s ^ 1]
        for step in range(1, far):
            for side in (core, 1 - core):
                row += [2 * at(chip, -step) + side, 2 * at(chip, step) + side]
        row += [2 * at(chip, far) + core, 2 * at(chip, far) + 1 - core]
        for side in (1 - core, core):
            row += [2 * (chip ^ k) + side for k in range(chips)]
        table.append(row)
    row = lax.dynamic_slice_in_dim(jnp.asarray(np.array(table, np.int32)), position, 1, 0)[0]
    first_slot = [0] + [2 + 4 * step for step in range(far)]

    half_rows = enc_rows.shape[0] // 2
    state = dec_input.astype(jnp.float32)
    normed = rms_scaled(state, dec_gain[0]).astype(jnp.bfloat16)
    queries = (
        jnp.einsum("td,hdk->htk", normed, w_query, preferred_element_type=jnp.float32) * score_scale
    ).astype(jnp.bfloat16)

    own = [prepare(position, enc_rows, enc_gain, 0)]
    own.append(prepare(position, enc_rows, enc_gain, 1, [queries, row]))

    carried = [None, None]
    slots = [[[(half, 0, half_rows)], [(swap(half), 0, half_rows)]] for half in own]
    held = [(half, half) for half in own]
    flying = [(hop(half, 1), hop(half, -1)) for half in own]
    token = own[1]
    for phase in range(2 * far):
        step, which = phase // 2 + 1, phase % 2
        *arrived, token = lax.optimization_barrier((*flying[phase], token))
        if step + 1 < far:
            flying.append((hop(arrived[0], 1), hop(arrived[1], -1)))
        elif step + 1 == far:
            cut = half_rows // 2
            flying.append((hop(arrived[0][:cut], 1), hop(arrived[1][cut:], -1)))
        other = swap(jnp.concatenate(arrived, axis=0))
        length = arrived[0].shape[0]
        if step < far:
            received = [[(part, 0, half_rows)] for part in arrived]
            received += [[(other, at, half_rows)] for at in (0, length)]
        else:
            rest = half_rows - length
            received = [
                [(arrived[0], 0, length), (arrived[1], 0, rest)],
                [(other, 0, length), (other, length, rest)],
            ]
        slots.append(received)
        if phase == 0:
            todo, half, begin = slots[0], 0, 0
        elif phase == 2:
            todo, half, begin = slots[1] + slots[3], 1, 0
        else:
            todo, half, begin = slots[phase + 1], 1 - which, first_slot[(phase + 1) // 2]
        if phase < 2 * far - 1:
            carried[half] = sum_step(row[begin : begin + len(todo)], todo, w_keyval, half_rows, carried[half])
            token = carried[half][1]
    last = first_slot[far]
    first = attend(row[last : last + 2], slots[2 * far], w_keyval, carried[0], queries)
    theirs, mine = attend(row[last:], slots[2 * far + 1], w_keyval, carried[1], queries, first, w_out, chips, cols)
    keep, *sends = split_blocks(mine, swap(theirs), PARTS)
    sends = [exchange(send, 2) for send in sends]
    parts = []
    for which, send in enumerate(sends):
        first, *others = fold_blocks(which, keep, send)
        lines = [*range(1, len(others)), 0]
        parts.append([first] + [exchange(others[line], 4 * (line + 1)) for line in lines])
    return finish(position, dec_input, parts)


def general_body(enc_rows, enc_gain, dec_input, dec_gain, w_query, w_keyval, w_out):
    sections = lax.axis_size("section")
    position = lax.axis_index("section")
    layers = dec_gain.shape[0]
    target_rows = dec_input.shape[0]
    model_width = dec_input.shape[1]
    head_size = w_query.shape[2]
    score_scale = 1.0 / math.sqrt(head_size)
    my_layer = position // (sections // layers)
    whole_rows = lax.all_gather(enc_rows, "section", axis=1, tiled=True)
    encoded = rms_scaled(whole_rows.astype(jnp.float32), enc_gain).astype(jnp.bfloat16)
    keyvals = jnp.einsum(
        "rd,hdk->rhk", encoded, w_keyval, preferred_element_type=jnp.float32
    ).astype(jnp.bfloat16)
    key_rows = keyvals[:, :, :head_size]
    value_rows = keyvals[:, :, head_size:]

    def head_context(normed):
        queries = (
            jnp.einsum("td,hdk->htk", normed, w_query, preferred_element_type=jnp.float32)
            * score_scale
        ).astype(jnp.bfloat16)
        scores = jnp.einsum("htk,rhk->htr", queries, key_rows, preferred_element_type=jnp.float32)
        weights_bf = jax.nn.softmax(scores, axis=-1).astype(jnp.bfloat16)
        return jnp.einsum(
            "htr,rhk->htk", weights_bf, value_rows, preferred_element_type=jnp.float32
        ).astype(jnp.bfloat16)

    col_share = model_width // sections
    col_start = position * col_share
    state_share = lax.dynamic_slice_in_dim(dec_input, col_start, col_share, 1).astype(jnp.float32)
    for layer_idx in range(layers):
        squares = lax.psum(jnp.sum(state_share * state_share, axis=1), "section")
        gain_share = lax.dynamic_slice_in_dim(dec_gain[layer_idx], col_start, col_share, 0)
        inverse = lax.rsqrt(squares / model_width + epsilon)
        normed_share = (state_share * inverse[:, None] * gain_share).astype(jnp.bfloat16)
        normed = lax.all_gather(normed_share, "section", axis=1, tiled=True)

        def project_out(normed_in):
            return jnp.einsum(
                "htk,hkd->td", head_context(normed_in), w_out, preferred_element_type=jnp.float32
            )

        def skipped(normed_in):
            return jnp.zeros((target_rows, model_width), jnp.float32)

        state_share = state_share + lax.psum_scatter(
            lax.cond(my_layer == layer_idx, project_out, skipped, normed),
            "section",
            scatter_dimension=1,
            tiled=True,
        )
    return state_share.astype(jnp.bfloat16)


def body(enc_rows, enc_gain, dec_input, dec_gain, w_query, w_keyval, w_out):
    chips, odd = divmod(lax.axis_size("section"), 2)
    ringed = not odd and 4 <= chips <= MAX_RING and chips & (chips - 1) == 0 and dec_gain.shape[0] == 1
    chosen = ring_body if ringed else general_body
    return chosen(enc_rows, enc_gain, dec_input, dec_gain, w_query, w_keyval, w_out)


def solution(mesh):
    in_specs = (
        P("groups", "section"),
        P(),
        P("groups", None),
        P(),
        P("section", None, None),
        P("section", None, None),
        P("section", None, None),
    )
    out_specs = P("groups", "section")
    return jax.shard_map(body, mesh=mesh, in_specs=in_specs, out_specs=out_specs, check_vma=False)
```
